1024 devices in a mesh: row: 32 (over y, z_hi), col: 32 (over x, z_lo, core).
Axes of the slice: x: 4, y: 8, z: 16 (z_hi: 4, z_lo: 4; z = z_hi * 4 + z_lo), core: 2. Of those that a mesh axis runs over, the one named last changes fastest.
Arguments:
- features: bfloat16 [131072, 256], P(('row', 'col')), may hold values from -6 to 6
- node_order: int32 [1024, 128], P(('row', 'col')), may hold values from 0 to 127, each once within a row
- tile_index: int32 [1024, 96], P(('row', 'col')), may hold values from 0 to 1023
- tile_count: int32 [1024], P(('row', 'col')), may hold values from 1 to 96, as said below
- tile_values: bfloat16 [1024, 96, 128, 128], P(('row', 'col')), may hold values from 0 to 0.022094727
- weight: bfloat16 [256, 256], replicated, may hold values from -0.375 to 0.375
- out_bias: float32 [256], replicated, may hold values from -3 to 3
- out_grad: bfloat16 [131072, 256], P(('row', 'col')), may hold values from -0.049560547 to 0.049560547
Outputs:
- activated: bfloat16 [131072, 256], P(('row', 'col'))
- weight_grad: float32 [256, 256], replicated
- bias_grad: float32 [256], replicated
The draws below stay inside these ranges and needn't reach their ends.
Inputs may be any that keep to these rules, and one draw needn't show every extreme that they name: `node_order`: each device's row is an ordering of 0 to 127. `tile_index`: positions may repeat within a device's slots. `tile_count`: some device uses all 96 slots.
All inputs are finite; a program needn't handle non-finite values.
Results may differ from the reference program's by a relative error of at most 0.0053.
Values may be sent and summed in bfloat16 or wider, within the bound.
No kernel may reach another device: no remote copies, remote signals or barrier semaphores. Data moves between devices by JAX's collectives and lax.ppermute only.
A program may use at most 64 MiB of HBM per device.

```python
import jax
import jax.numpy as jnp
from jax import lax

F = 256
TILE = 128
ROWS_DEV = 128
TILES = 96
NODES = 131072
GRID_OUT = 32
GRID_IN = 32
N_ROW = 32
N_COL = 32


def draw_tile_count(key, part):
    key = jax.random.fold_in(key, 11)
    key_shift, key_jitter, key_full = jax.random.split(key, 3)
    devices = N_ROW * N_COL
    shifts = jax.random.randint(key_shift, (devices,), 0, 4)
    jitter = jax.random.randint(key_jitter, (devices,), 0, TILES // 16 + 1)
    counts = jnp.maximum(TILES // jnp.left_shift(1, shifts) - jitter, 1)
    full_dev = jax.random.randint(key_full, (), 0, devices)
    counts = jnp.where(jnp.arange(devices) == full_dev, TILES, counts)
    return counts.astype(jnp.int32)


def place_ends(values, key, smallest, high):
    dims = values.shape
    place = [jax.random.randint(jax.random.fold_in(key, axis), (), 0, dims[axis]) for axis in range(len(dims))]
    values = values.at[tuple(place)].set(smallest)
    longest = dims.index(max(dims))
    place[longest] = (place[longest] + 1) % dims[longest]
    return values.at[tuple(place)].set(high)


def steps_of(key, shape, cuts, least, largest):
    factor_of, own = 1.0, jax.random.fold_in(key, 6)
    for dim, blocks in cuts:
        heights = jnp.exp(jax.random.uniform(jax.random.fold_in(own, dim), (blocks,), jnp.float32, least / len(cuts), largest / len(cuts)))
        factor_of = factor_of * jnp.repeat(heights, shape[dim] // blocks).reshape([-1 if axis == dim else 1 for axis in range(len(shape))])
    return factor_of


def bell_draw(own_key, shape, deviation, bound, shards=(), kind=jnp.bfloat16):
    result = deviation * jax.random.normal(own_key, shape, jnp.float32)
    if shards:
        result = result * steps_of(own_key, shape, shards, -0.22, 0.18)
    return jnp.clip(result, -bound, bound).astype(kind)


def setup_inputs(seed: int = 0) -> dict:
    key_of = jax.random.split(jax.random.key(seed), 9)
    return {
        "features": bell_draw(key_of[0], (NODES, F), 1.0, 6.0, ((0, 1024),)),
        "node_order": jax.vmap(lambda own: jax.random.permutation(own, ROWS_DEV))(jax.random.split(key_of[1], (N_ROW * N_COL))).reshape((N_ROW * N_COL, ROWS_DEV)).astype(jnp.int32),
        "tile_index": place_ends(jax.random.randint(key_of[2], (N_ROW * N_COL, TILES), 0, GRID_OUT * GRID_IN), jax.random.fold_in(key_of[2], 1), 0, (GRID_OUT * GRID_IN) - 1).astype(jnp.int32),
        "tile_count": draw_tile_count(jax.random.fold_in(key_of[8], 71), 0),
        "tile_values": jnp.clip(0.022094727 * jax.random.uniform(key_of[4], (N_ROW * N_COL, TILES, TILE, TILE), jnp.float32) ** steps_of(key_of[4], (N_ROW * N_COL, TILES, TILE, TILE), ((0, 1024),), -0.2, 0.2), 0.0, 0.022094727).astype(jnp.bfloat16),
        "weight": bell_draw(key_of[5], (F, F), F ** -0.5, 0.375),
        "out_bias": bell_draw(key_of[6], (F,), 0.5, 3.0, (), jnp.float32),
        "out_grad": bell_draw(key_of[7], (NODES, F), (3.0 * NODES ** -0.5), 0.049560547, ((0, 1024),)),
    }


def reference(features, node_order, tile_index, tile_count, tile_values, weight, out_bias, out_grad):
    devices = N_ROW * N_COL
    block_rows = N_COL * ROWS_DEV
    base = (jnp.arange(devices, dtype=jnp.int32) * ROWS_DEV)[:, None]
    perm_global = (base + node_order).reshape(-1).astype(jnp.int32)
    clustered = features[perm_global]
    by_group = clustered.reshape(N_ROW, N_COL, ROWS_DEV, F)
    slot_ids = jnp.arange(TILES, dtype=jnp.int32)
    grid_ids = jnp.arange(GRID_OUT, dtype=jnp.int32)

    def add_device(carry, device):
        row_pos = device // N_COL
        col_pos = device % N_COL
        source = lax.dynamic_index_in_dim(by_group, col_pos, 1, keepdims=False).reshape(GRID_IN, TILE, F)
        index_row = tile_index[device]
        tile_rows = index_row // GRID_IN
        tile_cols = index_row % GRID_IN
        gathered = source[tile_cols].astype(jnp.float32)
        prods = jnp.einsum('kab,kbf->kaf', tile_values[device].astype(jnp.float32), gathered,
                           precision=lax.Precision.HIGHEST)
        live = slot_ids < tile_count[device]
        onehot = ((tile_rows[:, None] == grid_ids[None, :]) & live[:, None]).astype(jnp.float32)
        partial_value = jnp.einsum('kg,kaf->gaf', onehot, prods, precision=lax.Precision.HIGHEST)
        partial_value = partial_value.reshape(block_rows, F)
        start = (row_pos * block_rows).astype(jnp.int32)
        current = lax.dynamic_slice_in_dim(carry, start, block_rows, 0)
        carry = lax.dynamic_update_slice_in_dim(carry, current + partial_value, start, 0)
        return carry, None

    aggregated, _ = lax.scan(add_device, jnp.zeros((NODES, F), jnp.float32),
                             jnp.arange(devices, dtype=jnp.int32))
    agg_round = aggregated.astype(jnp.bfloat16)
    pre_act = jnp.dot(agg_round, weight, preferred_element_type=jnp.float32) + out_bias
    sig = jax.nn.sigmoid(pre_act)
    act_clustered = (pre_act * sig).astype(jnp.bfloat16)
    activated = jnp.zeros((NODES, F), jnp.bfloat16).at[perm_global].set(act_clustered)
    grad_clustered = out_grad[perm_global].astype(jnp.float32)
    grad_pre = grad_clustered * sig * (1.0 + pre_act * (1.0 - sig))
    grad_round = grad_pre.astype(jnp.bfloat16)
    weight_grad = lax.dot_general(agg_round, grad_round, (((0,), (0,)), ((), ())),
                                  preferred_element_type=jnp.float32)
    bias_grad = jnp.sum(grad_pre, axis=0)
    return activated, weight_grad, bias_grad
```

```python
import jax
import jax.numpy as jnp
from jax import lax
from jax.experimental import pallas as pl
from jax.experimental.pallas import tpu as pltpu
from jax.sharding import Mesh, PartitionSpec as P

AXES = ("y", "zh", "x", "zl", "core")
COL = ("x", "zl", "core")
T = 128
F = 256
TILES = 96
GRID = 32
CHUNK = 16
UNROLL = 8
BF = jnp.bfloat16
F32 = jnp.float32


def cluster_body(order, feats, out):
    place = lax.broadcasted_iota(jnp.int32, (T, T), 0) == order[...]
    hot = place.astype(F32).astype(BF)
    out[...] = lax.dot_general(
        hot, feats[...], (((0,), (0,)), ((), ())), preferred_element_type=F32
    ).astype(BF)


def cluster(order, feats):
    return pl.pallas_call(
        cluster_body,
        out_shape=jax.ShapeDtypeStruct((T, F), BF),
        name="cluster",
    )(order, feats)


def tiles_body(me, index, count, *refs):
    tiles, pieces, out = refs[0], refs[1:10], refs[10]
    src, vals, acc, piece_sem, tile_sem = refs[11:]
    copies = []
    row = 0
    for i, piece in enumerate(pieces):
        rows = piece.shape[0]
        copies.append(pltpu.make_async_copy(piece, src.at[pl.ds(row, rows)], piece_sem.at[i]))
        row += rows
    loads = [
        pltpu.make_async_copy(tiles.at[pl.ds(c * CHUNK, CHUNK)], vals.at[pl.ds(c * CHUNK, CHUNK)], tile_sem.at[c])
        for c in range(TILES // CHUNK)
    ]
    for copy in copies + loads:
        copy.start()

    @pl.loop(0, GRID + 1)
    def _(r):
        acc[r] = jnp.zeros((T, F), F32)

    for copy in copies:
        copy.wait()
    used = count[0]
    here = me[0]
    for c, load in enumerate(loads):
        load.wait()

        @pl.loop(0, CHUNK // UNROLL)
        def _(g):
            first = c * CHUNK + g * UNROLL

            @pl.when(first < used)
            def _():
                for u in range(UNROLL):
                    k = first + u
                    at = index[0, k]
                    to = jnp.where(k < used, at // GRID, GRID)
                    col = at % GRID
                    slot = ((here - col // 4) & 7) * 4 + (col & 3)
                    start = pl.multiple_of(slot * T, T)
                    acc[to] += jnp.dot(vals[k], src[pl.ds(start, T), :], preferred_element_type=F32)

    @pl.loop(0, GRID)
    def _(r):
        out[(r & 1) * (GRID // 2) + (r >> 1)] = acc[r].astype(out.dtype)


def tile_sums(me, index, count, tiles, pieces):
    smem = pl.BlockSpec(memory_space=pltpu.SMEM)
    hbm = pl.BlockSpec(memory_space=pl.ANY)
    return pl.pallas_call(
        tiles_body,
        out_shape=jax.ShapeDtypeStruct((GRID, T, F), BF),
        in_specs=[smem] * 3 + [hbm] * (1 + len(pieces)),
        out_specs=pl.BlockSpec(memory_space=pltpu.VMEM),
        scratch_shapes=[
            pltpu.VMEM((GRID * T, F), BF),
            pltpu.VMEM((TILES, T, T), BF),
            pltpu.VMEM((GRID + 1, T, F), F32),
            pltpu.SemaphoreType.DMA((len(pieces),)),
            pltpu.SemaphoreType.DMA((TILES // CHUNK,)),
        ],
        compiler_params=pltpu.CompilerParams(vmem_limit_bytes=40 * 2**20),
        cost_estimate=pl.CostEstimate(
            flops=2 * TILES * T * T * F, bytes_accessed=8 * 2**20, transcendentals=0
        ),
        name="tile_sums",
    )(me, index, count, tiles, *pieces)


def finish_body(parts, order, weight, bias, out_grad, act_out, grads):
    total = parts[0].astype(F32)
    for i in range(1, parts.shape[0]):
        total += parts[i].astype(F32)
    agg = total.astype(BF)
    place = lax.broadcasted_iota(jnp.int32, (T, T), 0) == order[...]
    hot = place.astype(F32).astype(BF)
    pre = jnp.dot(agg, weight[...], preferred_element_type=F32) + bias[...]
    sig = jax.nn.sigmoid(pre)
    act = (pre * sig).astype(BF)
    act_out[...] = jnp.dot(hot, act, preferred_element_type=F32).astype(BF)
    cot = lax.dot_general(hot, out_grad[...], (((0,), (0,)), ((), ())), preferred_element_type=F32)
    grad = cot * sig * (1.0 + pre * (1.0 - sig))
    grads[:, :F] = lax.dot_general(
        agg, grad.astype(BF), (((0,), (0,)), ((), ())), preferred_element_type=F32
    )
    sums = jnp.sum(grad, axis=0, keepdims=True)
    grads[:, F:] = jnp.zeros((F, T), F32)
    grads[0:1, F:] = sums[:, :T]
    grads[8:9, F:] = sums[:, T:]


def finish(parts, order, weight, bias, out_grad):
    return pl.pallas_call(
        finish_body,
        out_shape=(jax.ShapeDtypeStruct((T, F), BF), jax.ShapeDtypeStruct((F, F + T), F32)),
        compiler_params=pltpu.CompilerParams(vmem_limit_bytes=40 * 2**20),
        name="finish",
    )(parts, order, weight, bias, out_grad)


def ring_gather(own):
    up = [(i, (i + 1) % 8) for i in range(8)]
    down = [(i, (i - 1) % 8) for i in range(8)]
    half = own.shape[0] // 2
    below, above = [own], [own]
    for _ in range(3):
        below.append(lax.ppermute(below[-1], "y", up))
        above.append(lax.ppermute(above[-1], "y", down))
    far = [lax.ppermute(below[-1][:half], "y", up), lax.ppermute(above[-1][half:], "y", down)]
    return below + far + above[:0:-1]


def local(features, node_order, tile_index, tile_count, tile_values, weight, out_bias, out_grad):
    clustered = cluster(node_order, features)
    near = lax.all_gather(clustered, "zh", axis=0, tiled=True)
    pieces = ring_gather(near)
    me = lax.axis_index("y").astype(jnp.int32).reshape(1)
    sums = tile_sums(me, tile_index, tile_count, tile_values[0], pieces)
    swapped = lax.all_to_all(sums, "core", 0, 0, tiled=True)
    half = GRID // 2
    paired = (swapped[:half].astype(F32) + swapped[half:].astype(F32)).astype(BF)
    parts = lax.all_to_all(paired, ("x", "zl"), 0, 0, tiled=True)
    activated, grads = finish(parts, node_order, weight, out_bias.reshape(1, F), out_grad)
    mine = lax.all_to_all(grads, COL, 0, 0, tiled=True).reshape(GRID, 8, F + T).sum(axis=0)
    mine = lax.psum(lax.psum(mine, "y"), "zh")
    whole = lax.all_to_all(jnp.tile(mine, (GRID, 1)), COL, 0, 0, tiled=True)
    bias_grad = jnp.concatenate([whole[0, F:], whole[8, F:]])
    return activated, whole[:, :F], bias_grad


def solution(mesh):
    fine = Mesh(mesh.devices.reshape(8, 4, 4, 4, 2), AXES)
    return jax.shard_map(
        local,
        mesh=fine,
        in_specs=(
            P(AXES, None),
            P(AXES, None),
            P(AXES, None),
            P(AXES),
            P(AXES, None, None, None),
            P(),
            P(),
            P(AXES, None),
        ),
        out_specs=(P(AXES, None), P(), P()),
        check_vma=False,
    )
```

```python
import jax
import jax.numpy as jnp
from jax import lax
from jax.experimental import pallas as pl
from jax.experimental.pallas import tpu as pltpu
from jax.sharding import Mesh, PartitionSpec as P

AXES = ("y", "zh", "x", "zl", "core")
T = 128
F = 256
TILES = 96
GRID = 32
CHUNK = 16
UNROLL = 8
BF = jnp.bfloat16
F32 = jnp.float32


def cluster_body(order, feats, out):
    place = lax.broadcasted_iota(jnp.int32, (T, T), 0) == order[...]
    hot = place.astype(F32).astype(BF)
    out[...] = lax.dot_general(
        hot, feats[...], (((0,), (0,)), ((), ())), preferred_element_type=F32
    ).astype(BF)


def cluster(order, feats):
    return pl.pallas_call(
        cluster_body,
        out_shape=jax.ShapeDtypeStruct((T, F), BF),
        name="cluster",
    )(order, feats)


def tiles_body(spot, index, count, *refs):
    tiles, pieces, mine, other = refs[0], refs[1:10], refs[10], refs[11]
    src, vals, acc, piece_sem, tile_sem = refs[12:]
    copies = []
    row = 0
    for i, piece in enumerate(pieces):
        rows = piece.shape[0]
        copies.append(pltpu.make_async_copy(piece, src.at[pl.ds(row, rows)], piece_sem.at[i]))
        row += rows
    loads = [
        pltpu.make_async_copy(tiles.at[pl.ds(c * CHUNK, CHUNK)], vals.at[pl.ds(c * CHUNK, CHUNK)], tile_sem.at[c])
        for c in range(TILES // CHUNK)
    ]
    for copy in copies + loads:
        copy.start()

    @pl.loop(0, GRID + 1)
    def _(r):
        acc[r] = jnp.zeros((T, F), F32)

    for copy in copies:
        copy.wait()
    used = count[0]
    here, core = spot[0], spot[1]
    for c, load in enumerate(loads):
        load.wait()

        @pl.loop(0, CHUNK // UNROLL)
        def _(g):
            first = c * CHUNK + g * UNROLL

            @pl.when(first < used)
            def _():
                for u in range(UNROLL):
                    k = first + u
                    at = index[0, k]
                    to = jnp.where(k < used, at // GRID, GRID)
                    col = at % GRID
                    slot = ((here - col // 4) & 7) * 4 + (col & 3)
                    start = pl.multiple_of(slot * T, T)
                    acc[to] += jnp.dot(vals[k], src[pl.ds(start, T), :], preferred_element_type=F32)

    @pl.loop(0, GRID // 2)
    def _(r):
        other[r] = acc[2 * r + 1 - core].astype(other.dtype)
        mine[r] = acc[2 * r + core]


def tile_sums(spot, index, count, tiles, pieces):
    smem = pl.BlockSpec(memory_space=pltpu.SMEM)
    hbm = pl.BlockSpec(memory_space=pl.ANY)
    return pl.pallas_call(
        tiles_body,
        out_shape=(
            jax.ShapeDtypeStruct((GRID // 2, T, F), F32),
            jax.ShapeDtypeStruct((GRID // 2, T, F), BF),
        ),
        in_specs=[smem] * 3 + [pl.BlockSpec(memory_space=pltpu.HBM)] + [hbm] * len(pieces),
        out_specs=[pl.BlockSpec(memory_space=pltpu.VMEM)] * 2,
        scratch_shapes=[
            pltpu.VMEM((GRID * T, F), BF),
            pltpu.VMEM((TILES, T, T), BF),
            pltpu.VMEM((GRID + 1, T, F), F32),
            pltpu.SemaphoreType.DMA((len(pieces),)),
            pltpu.SemaphoreType.DMA((TILES // CHUNK,)),
        ],
        compiler_params=pltpu.CompilerParams(vmem_limit_bytes=50 * 2**20),
        cost_estimate=pl.CostEstimate(
            flops=2 * TILES * T * T * F, bytes_accessed=8 * 2**20, transcendentals=0
        ),
        name="tile_sums",
    )(spot, index, count, tiles, *pieces)


def finish_body(core, parts, order, weight, bias, out_grad, act_out, mine, other):
    total = parts[0].astype(F32)
    for i in range(1, parts.shape[0]):
        total += parts[i].astype(F32)
    agg = total.astype(BF)
    place = lax.broadcasted_iota(jnp.int32, (T, T), 0) == order[...]
    hot = place.astype(F32).astype(BF)
    pre = jnp.dot(agg, weight[...], preferred_element_type=F32) + bias[...]
    sig = jax.nn.sigmoid(pre)
    act = (pre * sig).astype(BF)
    act_out[...] = jnp.dot(hot, act, preferred_element_type=F32).astype(BF)
    cot = lax.dot_general(hot, out_grad[...], (((0,), (0,)), ((), ())), preferred_element_type=F32)
    grad = cot * sig * (1.0 + pre * (1.0 - sig))
    wgrad = lax.dot_general(
        agg, grad.astype(BF), (((0,), (0,)), ((), ())), preferred_element_type=F32
    )
    sums = jnp.sum(grad, axis=0, keepdims=True)
    first = core[0] == 0

    def halves(lead, low, high):
        return (jnp.where(lead, low, high), jnp.where(lead, high, low))

    own, away = halves(first, wgrad[:T], wgrad[T:])
    own_sum, away_sum = halves(first, sums[:, :T], sums[:, T:])
    for out, half, tail in ((mine, own, own_sum), (other, away, away_sum)):
        out[:, 8:, :] = jnp.zeros((GRID, 8, T), F32)
        out[0, 8:9, :] = tail
        for i in range(T // 8):
            for h in range(2):
                out[2 * i + h, :8, :] = half[8 * i : 8 * i + 8, T * h : T * h + T]


def finish(core, parts, order, weight, bias, out_grad):
    smem = pl.BlockSpec(memory_space=pltpu.SMEM)
    vmem = pl.BlockSpec(memory_space=pltpu.VMEM)
    return pl.pallas_call(
        finish_body,
        out_shape=(
            jax.ShapeDtypeStruct((T, F), BF),
            jax.ShapeDtypeStruct((GRID, 16, T), F32),
            jax.ShapeDtypeStruct((GRID, 16, T), F32),
        ),
        in_specs=[smem] + [vmem] * 5,
        out_specs=[vmem] * 3,
        compiler_params=pltpu.CompilerParams(vmem_limit_bytes=40 * 2**20),
        name="finish",
    )(core, parts, order, weight, bias, out_grad)


def unpack_body(core, mine, other, wgrad, bgrad):
    first = core[0] == 0
    for c in range(2):
        pick = first if c == 0 else jnp.logical_not(first)
        for i in range(T // 8):
            for h in range(2):
                wgrad[T * c + 8 * i : T * c + 8 * i + 8, T * h : T * h + T] = jnp.where(
                    pick, mine[2 * i + h, :8, :], other[2 * i + h, :8, :]
                )
        bgrad[:, T * c : T * c + T] = jnp.where(pick, mine[0, 8:9, :], other[0, 8:9, :])


def unpack(core, mine, other):
    smem = pl.BlockSpec(memory_space=pltpu.SMEM)
    vmem = pl.BlockSpec(memory_space=pltpu.VMEM)
    return pl.pallas_call(
        unpack_body,
        out_shape=(jax.ShapeDtypeStruct((F, F), F32), jax.ShapeDtypeStruct((1, F), F32)),
        in_specs=[smem, vmem, vmem],
        out_specs=[vmem] * 2,
        name="unpack",
    )(core, mine, other)


def ring_gather(own):
    up = [(i, (i + 1) % 8) for i in range(8)]
    down = [(i, (i - 1) % 8) for i in range(8)]
    half = own.shape[0] // 2
    below, above = [own], [own]
    for _ in range(3):
        below.append(lax.ppermute(below[-1], "y", up))
        above.append(lax.ppermute(above[-1], "y", down))
    far = [lax.ppermute(below[-1][:half], "y", up), lax.ppermute(above[-1][half:], "y", down)]
    return below + far + above[:0:-1]


def spread(block, axes, copies):
    repeated = jnp.broadcast_to(block[None], (copies, *block.shape))
    return lax.all_to_all(repeated, axes, 0, 0, tiled=True)


def local(features, node_order, tile_index, tile_count, tile_values, weight, out_bias, out_grad):
    swap = [(0, 1), (1, 0)]
    row_at = lax.axis_index("y").astype(jnp.int32)
    core = lax.axis_index("core").astype(jnp.int32)
    clustered = cluster(node_order, features)
    near = lax.all_gather(clustered, "zh", axis=0, tiled=True)
    pieces = ring_gather(near)
    mine, other = tile_sums(
        jnp.stack([row_at, core]), tile_index, tile_count, tile_values[0], pieces
    )
    paired = (mine + lax.ppermute(other, "core", swap).astype(F32)).astype(BF)
    parts = lax.all_to_all(paired, ("x", "zl"), 0, 0, tiled=True)
    core = core.reshape(1)
    activated, mine, other = finish(
        core, parts, node_order, weight, out_bias.reshape(1, F), out_grad
    )
    half = mine + lax.ppermute(other, "core", swap)
    block = lax.all_to_all(half, ("y", "x"), 0, 0, tiled=True).sum(axis=0)
    block = spread(block, ("zh", "zl"), 16).sum(axis=0)
    half = spread(block, ("y", "x"), GRID)
    weight_grad, bias_grad = unpack(core, half, lax.ppermute(half, "core", swap))
    return activated, weight_grad, bias_grad.reshape(F)


def solution(mesh):
    fine = Mesh(mesh.devices.reshape(8, 4, 4, 4, 2), AXES)
    return jax.shard_map(
        local,
        mesh=fine,
        in_specs=(
            P(AXES, None),
            P(AXES, None),
            P(AXES, None),
            P(AXES),
            P(AXES, None, None, None),
            P(),
            P(),
            P(AXES, None),
        ),
        out_specs=(P(AXES, None), P(), P()),
        check_vma=False,
    )
```

```python
import jax
import jax.numpy as jnp
from jax import lax
from jax.experimental import pallas as pl
from jax.experimental.pallas import tpu as pltpu
from jax.sharding import Mesh, PartitionSpec as P

AXES = ("y", "zh", "x", "zl", "core")
T = 128
F = 256
TILES = 96
GRID = 32
CHUNK = 16
UNROLL = 8
BF = jnp.bfloat16
F32 = jnp.float32


def cluster_body(order, feats, out):
    place = lax.broadcasted_iota(jnp.int32, (T, T), 0) == order[...]
    hot = place.astype(F32).astype(BF)
    out[...] = lax.dot_general(
        hot, feats[...], (((0,), (0,)), ((), ())), preferred_element_type=F32
    ).astype(BF)


def cluster(order, feats):
    return pl.pallas_call(
        cluster_body,
        out_shape=jax.ShapeDtypeStruct((T, F), BF),
        name="cluster",
    )(order, feats)


def tiles_body(ints, *refs):
    tiles, pieces, mine, other = refs[0], refs[1:10], refs[10], refs[11]
    src, vals, acc, piece_sem, tile_sem = refs[12:]
    copies = []
    row = 0
    for i, piece in enumerate(pieces):
        rows = piece.shape[0]
        copies.append(pltpu.make_async_copy(piece, src.at[pl.ds(row, rows)], piece_sem.at[i]))
        row += rows
    loads = [
        pltpu.make_async_copy(tiles.at[pl.ds(c * CHUNK, CHUNK)], vals.at[pl.ds(c * CHUNK, CHUNK)], tile_sem.at[c])
        for c in range(TILES // CHUNK)
    ]
    for copy in copies + loads:
        copy.start()

    @pl.loop(0, GRID + 1)
    def _(r):
        acc[r] = jnp.zeros((T, F), F32)

    for copy in copies:
        copy.wait()
    used, here, core = ints[TILES], ints[TILES + 1], ints[TILES + 2]
    for c, load in enumerate(loads):
        load.wait()

        @pl.loop(0, CHUNK // UNROLL)
        def _(g):
            first = c * CHUNK + g * UNROLL

            @pl.when(first < used)
            def _():
                for u in range(UNROLL):
                    k = first + u
                    at = ints[k]
                    to = jnp.where(k < used, at // GRID, GRID)
                    col = at % GRID
                    slot = ((here - col // 4) & 7) * 4 + (col & 3)
                    start = pl.multiple_of(slot * T, T)
                    acc[to] += jnp.dot(vals[k], src[pl.ds(start, T), :], preferred_element_type=F32)

    @pl.loop(0, GRID // 2)
    def _(r):
        other[r] = acc[2 * r + 1 - core].astype(other.dtype)
        mine[r] = acc[2 * r + core]


def tile_sums(ints, tiles, pieces):
    smem = pl.BlockSpec(memory_space=pltpu.SMEM)
    hbm = pl.BlockSpec(memory_space=pl.ANY)
    return pl.pallas_call(
        tiles_body,
        out_shape=(
            jax.ShapeDtypeStruct((GRID // 2, T, F), F32),
            jax.ShapeDtypeStruct((GRID // 2, T, F), BF),
        ),
        in_specs=[smem] + [hbm] * (1 + len(pieces)),
        out_specs=[pl.BlockSpec(memory_space=pltpu.VMEM)] * 2,
        scratch_shapes=[
            pltpu.VMEM((GRID * T, F), BF),
            pltpu.VMEM((TILES, T, T), BF),
            pltpu.VMEM((GRID + 1, T, F), F32),
            pltpu.SemaphoreType.DMA((len(pieces),)),
            pltpu.SemaphoreType.DMA((TILES // CHUNK,)),
        ],
        compiler_params=pltpu.CompilerParams(vmem_limit_bytes=47 * 2**20),
        cost_estimate=pl.CostEstimate(
            flops=2 * TILES * T * T * F, bytes_accessed=8 * 2**20, transcendentals=0
        ),
        name="tile_sums",
    )(ints, tiles, *pieces)


def finish_body(core, parts, order, weight, bias, out_grad, act_out, mine, other):
    total = parts[0].astype(F32)
    for i in range(1, parts.shape[0]):
        total += parts[i].astype(F32)
    agg = total.astype(BF)
    place = lax.broadcasted_iota(jnp.int32, (T, T), 0) == order[...]
    hot = place.astype(F32).astype(BF)
    pre = jnp.dot(agg, weight[...], preferred_element_type=F32) + bias[...]
    sig = jax.nn.sigmoid(pre)
    act = (pre * sig).astype(BF)
    act_out[...] = jnp.dot(hot, act, preferred_element_type=F32).astype(BF)
    cot = lax.dot_general(hot, out_grad[...], (((0,), (0,)), ((), ())), preferred_element_type=F32)
    grad = cot * sig * (1.0 + pre * (1.0 - sig))
    wgrad = lax.dot_general(
        agg, grad.astype(BF), (((0,), (0,)), ((), ())), preferred_element_type=F32
    )
    sums = jnp.sum(grad, axis=0, keepdims=True)
    first = core[0] == 0

    def halves(lead, low, high):
        return (jnp.where(lead, low, high), jnp.where(lead, high, low))

    own, away = halves(first, wgrad[:T], wgrad[T:])
    own_sum, away_sum = halves(first, sums[:, :T], sums[:, T:])
    for out, half, tail in ((mine, own, own_sum), (other, away, away_sum)):
        out[:, 0, 4 * F :] = jnp.zeros((GRID, T), F32)
        out[0:1, 0, 4 * F :] = tail
        for q in range(4):
            out[:, 0, q * F : (q + 1) * F] = half[q * GRID : (q + 1) * GRID]


def finish(core, parts, order, weight, bias, out_grad):
    smem = pl.BlockSpec(memory_space=pltpu.SMEM)
    vmem = pl.BlockSpec(memory_space=pltpu.VMEM)
    return pl.pallas_call(
        finish_body,
        out_shape=(
            jax.ShapeDtypeStruct((T, F), BF),
            jax.ShapeDtypeStruct((GRID, 1, 4 * F + T), F32),
            jax.ShapeDtypeStruct((GRID, 1, 4 * F + T), F32),
        ),
        in_specs=[smem] + [vmem] * 5,
        out_specs=[vmem] * 3,
        compiler_params=pltpu.CompilerParams(vmem_limit_bytes=40 * 2**20),
        name="finish",
    )(core, parts, order, weight, bias, out_grad)


def unpack_body(core, mine, other, wgrad, bgrad):
    first = core[0] == 0
    for c in range(2):
        pick = first if c == 0 else jnp.logical_not(first)
        for q in range(4):
            at = T * c + GRID * q
            lanes = slice(q * F, (q + 1) * F)
            wgrad[at : at + GRID, :] = jnp.where(pick, mine[:, 0, lanes], other[:, 0, lanes])
        bgrad[:, T * c : T * c + T] = jnp.where(pick, mine[0:1, 0, 4 * F :], other[0:1, 0, 4 * F :])


def unpack(core, mine, other):
    smem = pl.BlockSpec(memory_space=pltpu.SMEM)
    vmem = pl.BlockSpec(memory_space=pltpu.VMEM)
    return pl.pallas_call(
        unpack_body,
        out_shape=(jax.ShapeDtypeStruct((F, F), F32), jax.ShapeDtypeStruct((1, F), F32)),
        in_specs=[smem, vmem, vmem],
        out_specs=[vmem] * 2,
        compiler_params=pltpu.CompilerParams(vmem_limit_bytes=16 * 2**20),
        name="unpack",
    )(core, mine, other)


def ring_gather(own):
    up = [(i, (i + 1) % 8) for i in range(8)]
    down = [(i, (i - 1) % 8) for i in range(8)]
    half = own.shape[0] // 2
    below, above = [own], [own]
    for _ in range(3):
        below.append(lax.ppermute(below[-1], "y", up))
        above.append(lax.ppermute(above[-1], "y", down))
    far = [lax.ppermute(below[-1][:half], "y", up), lax.ppermute(above[-1][half:], "y", down)]
    return below + far + above[:0:-1]


def spread(block, axes, copies):
    repeated = jnp.broadcast_to(block[None], (copies, *block.shape))
    return lax.all_to_all(repeated, axes, 0, 0, tiled=True)


def local(features, node_order, tile_index, tile_count, tile_values, weight, out_bias, out_grad):
    swap = [(0, 1), (1, 0)]
    row_at = lax.axis_index("y").astype(jnp.int32)
    core = lax.axis_index("core").astype(jnp.int32)
    clustered = cluster(node_order, features)
    near = lax.all_gather(clustered, "zh", axis=0, tiled=True)
    pieces = ring_gather(near)
    ints = jnp.concatenate([tile_index[0], tile_count, jnp.stack([row_at, core])])
    mine, other = tile_sums(ints, tile_values[0], pieces)
    paired = (mine + lax.ppermute(other, "core", swap).astype(F32)).astype(BF)
    parts = lax.all_to_all(paired, ("x", "zl"), 0, 0, tiled=True)
    core = core.reshape(1)
    activated, mine, other = finish(
        core, parts, node_order, weight, out_bias.reshape(1, F), out_grad
    )
    half = mine + lax.ppermute(other, "core", swap)
    block = lax.all_to_all(half, ("y", "x"), 0, 0, tiled=True).sum(axis=0)
    block = spread(block, ("zh", "zl"), 16).sum(axis=0)
    half = spread(block, ("y", "x"), GRID)
    weight_grad, bias_grad = unpack(core, half, lax.ppermute(half, "core", swap))
    return activated, weight_grad, bias_grad.reshape(F)


def solution(mesh):
    fine = Mesh(mesh.devices.reshape(8, 4, 4, 4, 2), AXES)
    return jax.shard_map(
        local,
        mesh=fine,
        in_specs=(
            P(AXES, None),
            P(AXES, None),
            P(AXES, None),
            P(AXES),
            P(AXES, None, None, None),
            P(),
            P(),
            P(AXES, None),
        ),
        out_specs=(P(AXES, None), P(), P()),
        check_vma=False,
    )
```

```python
import jax
import jax.numpy as jnp
from jax import lax
from jax.experimental import pallas as pl
from jax.experimental.pallas import tpu as pltpu
from jax.sharding import Mesh, PartitionSpec as P

AXES = ("y", "zh", "x", "zl", "core")
T = 128
F = 256
TILES = 96
GRID = 32
UNROLL = 8
FAR_FROM, FAR_TO = 3, 6
NEAR_ROWS = (0, 512, 1024, 3072, 3584)
FAR_ROWS = (1536, 2048, 2304, 2560)
BF = jnp.bfloat16
F32 = jnp.float32


def cluster_body(order, feats, out):
    place = lax.broadcasted_iota(jnp.int32, (T, T), 0) == order[...]
    hot = place.astype(F32).astype(BF)
    out[...] = lax.dot_general(
        hot, feats[...], (((0,), (0,)), ((), ())), preferred_element_type=F32
    ).astype(BF)


def cluster(order, feats):
    return pl.pallas_call(
        cluster_body,
        out_shape=jax.ShapeDtypeStruct((T, F), BF),
        name="cluster",
    )(order, feats)


def near_block(ints, k):
    at = ints[k]
    row, col = at // GRID, at % GRID
    back = (ints[TILES + 1] - col // 4) & 7
    start = pl.multiple_of((back * 4 + (col & 3)) * T, T)
    to = ((row & 1) ^ ints[TILES + 2]) * (GRID // 2) + (row >> 1)
    return jnp.logical_or(back < FAR_FROM, back >= FAR_TO), start, to


def add_tiles(ints, listed, used, vals, src, acc):
    @pl.loop(0, (used + UNROLL - 1) // UNROLL)
    def _(g):
        for u in range(UNROLL):
            i = g * UNROLL + u
            k = jnp.where(i < used, listed[i], 0)
            _, start, to = near_block(ints, k)
            to = jnp.where(i < used, to, GRID)
            acc[to] += jnp.dot(vals[k], src[pl.ds(start, T), :], preferred_element_type=F32)


def first_body(ints, *refs):
    vals, pieces, acc, later = refs[0], refs[1:-5], refs[-5], refs[-4]
    src, now, piece_sem = refs[-3:]
    copies = []
    for i, (piece, row) in enumerate(zip(pieces, NEAR_ROWS)):
        copies.append(pltpu.make_async_copy(piece, src.at[pl.ds(row, piece.shape[0])], piece_sem.at[i]))
    for copy in copies:
        copy.start()

    @pl.loop(0, GRID + 1)
    def _(r):
        acc[r] = jnp.zeros((T, F), F32)

    def sort(k, counts):
        near, _, _ = near_block(ints, k)
        early, late = counts
        now[early] = k
        later[late] = k
        step = near.astype(jnp.int32)
        return early + step, late + 1 - step

    early, late = lax.fori_loop(0, ints[TILES], sort, (jnp.int32(0), jnp.int32(0)))
    later[TILES + 1] = late
    for copy in copies:
        copy.wait()
    add_tiles(ints, now, early, vals, src, acc)


def first_sums(ints, tiles, pieces):
    smem = pl.BlockSpec(memory_space=pltpu.SMEM)
    vmem = pl.BlockSpec(memory_space=pltpu.VMEM)
    hbm = pl.BlockSpec(memory_space=pl.ANY)
    return pl.pallas_call(
        first_body,
        out_shape=(
            jax.ShapeDtypeStruct((GRID + 1, T, F), F32),
            jax.ShapeDtypeStruct((T,), jnp.int32),
        ),
        in_specs=[smem, vmem] + [hbm] * len(pieces),
        out_specs=[vmem, smem],
        scratch_shapes=[
            pltpu.VMEM((GRID * T, F), BF),
            pltpu.SMEM((T,), jnp.int32),
            pltpu.SemaphoreType.DMA((len(pieces),)),
        ],
        compiler_params=pltpu.CompilerParams(vmem_limit_bytes=24 * 2**20),
        cost_estimate=pl.CostEstimate(
            flops=2 * TILES * T * T * F, bytes_accessed=8 * 2**20, transcendentals=0
        ),
        name="first_sums",
    )(ints, tiles, *pieces)


def last_body(ints, listed, begun, vals, *refs):
    pieces, mine, other = refs[:-5], refs[-5], refs[-4]
    src, acc, piece_sem = refs[-3:]
    copies = []
    for i, (piece, row) in enumerate(zip(pieces, FAR_ROWS)):
        copies.append(pltpu.make_async_copy(piece, src.at[pl.ds(row, piece.shape[0])], piece_sem.at[i]))
    for copy in copies:
        copy.start()

    @pl.loop(0, GRID + 1)
    def _(r):
        acc[r] = begun[r]

    for copy in copies:
        copy.wait()
    add_tiles(ints, listed, listed[TILES + 1], vals, src, acc)

    @pl.loop(0, GRID // 2)
    def _(r):
        mine[r] = acc[r]
        other[r] = acc[GRID // 2 + r].astype(other.dtype)


def last_sums(ints, listed, begun, vals, pieces):
    smem = pl.BlockSpec(memory_space=pltpu.SMEM)
    vmem = pl.BlockSpec(memory_space=pltpu.VMEM)
    hbm = pl.BlockSpec(memory_space=pl.ANY)
    return pl.pallas_call(
        last_body,
        out_shape=(
            jax.ShapeDtypeStruct((GRID // 2, T, F), F32),
            jax.ShapeDtypeStruct((GRID // 2, T, F), BF),
        ),
        in_specs=[smem, smem, vmem, vmem] + [hbm] * len(pieces),
        out_specs=[vmem] * 2,
        scratch_shapes=[
            pltpu.VMEM((GRID * T, F), BF),
            pltpu.VMEM((GRID + 1, T, F), F32),
            pltpu.SemaphoreType.DMA((len(pieces),)),
        ],
        compiler_params=pltpu.CompilerParams(vmem_limit_bytes=24 * 2**20),
        cost_estimate=pl.CostEstimate(
            flops=TILES * T * T * F, bytes_accessed=8 * 2**20, transcendentals=0
        ),
        name="last_sums",
    )(ints, listed, begun, vals, *pieces)


def finish_body(core, parts, order, weight, bias, out_grad, act_out, mine, other):
    total = parts[0].astype(F32)
    for i in range(1, parts.shape[0]):
        total += parts[i].astype(F32)
    agg = total.astype(BF)
    place = lax.broadcasted_iota(jnp.int32, (T, T), 0) == order[...]
    hot = place.astype(F32).astype(BF)
    pre = jnp.dot(agg, weight[...], preferred_element_type=F32) + bias[...]
    sig = jax.nn.sigmoid(pre)
    act = (pre * sig).astype(BF)
    act_out[...] = jnp.dot(hot, act, preferred_element_type=F32).astype(BF)
    cot = lax.dot_general(hot, out_grad[...], (((0,), (0,)), ((), ())), preferred_element_type=F32)
    grad = cot * sig * (1.0 + pre * (1.0 - sig))
    wgrad = lax.dot_general(
        agg, grad.astype(BF), (((0,), (0,)), ((), ())), preferred_element_type=F32
    )
    sums = jnp.sum(grad, axis=0, keepdims=True)
    first = core[0] == 0

    def halves(lead, low, high):
        return (jnp.where(lead, low, high), jnp.where(lead, high, low))

    own, away = halves(first, wgrad[:T], wgrad[T:])
    own_sum, away_sum = halves(first, sums[:, :T], sums[:, T:])
    for out, half, tail in ((mine, own, own_sum), (other, away, away_sum)):
        out[:, 0, 4 * F :] = jnp.zeros((GRID, T), F32)
        out[0:1, 0, 4 * F :] = tail
        for q in range(4):
            out[:, 0, q * F : (q + 1) * F] = half[q * GRID : (q + 1) * GRID]


def finish(core, parts, order, weight, bias, out_grad):
    smem = pl.BlockSpec(memory_space=pltpu.SMEM)
    vmem = pl.BlockSpec(memory_space=pltpu.VMEM)
    return pl.pallas_call(
        finish_body,
        out_shape=(
            jax.ShapeDtypeStruct((T, F), BF),
            jax.ShapeDtypeStruct((GRID, 1, 4 * F + T), F32),
            jax.ShapeDtypeStruct((GRID, 1, 4 * F + T), F32),
        ),
        in_specs=[smem] + [vmem] * 5,
        out_specs=[vmem] * 3,
        compiler_params=pltpu.CompilerParams(vmem_limit_bytes=40 * 2**20),
        name="finish",
    )(core, parts, order, weight, bias, out_grad)


def unpack_body(core, mine, other, wgrad, bgrad):
    first = core[0] == 0
    for c in range(2):
        pick = first if c == 0 else jnp.logical_not(first)
        for q in range(4):
            at = T * c + GRID * q
            lanes = slice(q * F, (q + 1) * F)
            wgrad[at : at + GRID, :] = jnp.where(pick, mine[:, 0, lanes], other[:, 0, lanes])
        bgrad[:, T * c : T * c + T] = jnp.where(pick, mine[0:1, 0, 4 * F :], other[0:1, 0, 4 * F :])


def unpack(core, mine, other):
    smem = pl.BlockSpec(memory_space=pltpu.SMEM)
    vmem = pl.BlockSpec(memory_space=pltpu.VMEM)
    return pl.pallas_call(
        unpack_body,
        out_shape=(jax.ShapeDtypeStruct((F, F), F32), jax.ShapeDtypeStruct((1, F), F32)),
        in_specs=[smem, vmem, vmem],
        out_specs=[vmem] * 2,
        compiler_params=pltpu.CompilerParams(vmem_limit_bytes=16 * 2**20),
        name="unpack",
    )(core, mine, other)


def ring_gather(own):
    def shift(block, by):
        return lax.ppermute(block, "y", [(i, (i + by) % 8) for i in range(8)])

    half = own.shape[0] // 2
    back1, ahead1, back2, ahead2 = (shift(own, by) for by in (1, -1, 2, -2))
    back3, ahead3 = shift(back2, 1), shift(ahead2, -1)
    far_low, far_high = shift(back2[:half], 2), shift(ahead2[half:], -2)
    return (own, back1, back2, ahead2, ahead1), (back3, far_low, far_high, ahead3)


def spread(block, axes, copies):
    repeated = jnp.broadcast_to(block[None], (copies, *block.shape))
    return lax.all_to_all(repeated, axes, 0, 0, tiled=True)


def local(features, node_order, tile_index, tile_count, tile_values, weight, out_bias, out_grad):
    swap = [(0, 1), (1, 0)]
    row_at = lax.axis_index("y").astype(jnp.int32)
    core = lax.axis_index("core").astype(jnp.int32)
    clustered = cluster(node_order, features)
    near = lax.all_gather(clustered, "zh", axis=0, tiled=True)
    early, late = ring_gather(near)
    ints = jnp.concatenate([tile_index[0], tile_count, jnp.stack([row_at, core])])
    begun, listed = first_sums(ints, tile_values[0], early)
    mine, other = last_sums(ints, listed, begun, tile_values[0], late)
    paired = (mine + lax.ppermute(other, "core", swap).astype(F32)).astype(BF)
    parts = lax.all_to_all(paired, ("x", "zl"), 0, 0, tiled=True)
    core = core.reshape(1)
    activated, mine, other = finish(
        core, parts, node_order, weight, out_bias.reshape(1, F), out_grad
    )
    half = mine + lax.ppermute(other, "core", swap)
    block = lax.all_to_all(half, ("y", "x"), 0, 0, tiled=True).sum(axis=0)
    block = spread(block, ("zh", "zl"), 16).sum(axis=0)
    half = spread(block, ("y", "x"), GRID)
    weight_grad, bias_grad = unpack(core, half, lax.ppermute(half, "core", swap))
    return activated, weight_grad, bias_grad.reshape(F)


def solution(mesh):
    fine = Mesh(mesh.devices.reshape(8, 4, 4, 4, 2), AXES)
    return jax.shard_map(
        local,
        mesh=fine,
        in_specs=(
            P(AXES, None),
            P(AXES, None),
            P(AXES, None),
            P(AXES),
            P(AXES, None, None, None),
            P(),
            P(),
            P(AXES, None),
        ),
        out_specs=(P(AXES, None), P(), P()),
        check_vma=False,
    )
```

```python
import functools

import jax
import jax.numpy as jnp
from jax import lax
from jax.experimental import pallas as pl
from jax.experimental.pallas import tpu as pltpu
from jax.sharding import Mesh, PartitionSpec as P

AXES = ("y", "zh", "x", "zl", "core")
T = 128
F = 256
TILES = 96
GRID = 32
UNROLL = 8
FAR_FROM, FAR_TO = 3, 6
NEAR_ROWS = (0, 512, 1024, 3072, 3584)
FAR_ROWS = (1536, 2048, 2304, 2560)
BF = jnp.bfloat16
F32 = jnp.float32


def cluster_body(order, feats, out):
    place = lax.broadcasted_iota(jnp.int32, (T, T), 0) == order[...]
    hot = place.astype(F32).astype(BF)
    out[...] = lax.dot_general(
        hot, feats[...], (((0,), (0,)), ((), ())), preferred_element_type=F32
    ).astype(BF)


def cluster(order, feats):
    return pl.pallas_call(
        cluster_body,
        out_shape=jax.ShapeDtypeStruct((T, F), BF),
        name="cluster",
    )(order, feats)


def add_tiles(listed, vals, src, acc, base):
    used, spare = listed[TILES + 1], acc.shape[0] - 1

    @pl.loop(0, (used + UNROLL - 1) // UNROLL)
    def _(g):
        for u in range(UNROLL):
            i = g * UNROLL + u
            entry = listed[i]
            to = jnp.where(i < used, (entry >> 12) - base, spare)
            k = jnp.where(i < used, entry & 127, 0)
            start = pl.multiple_of(jnp.where(i < used, (entry >> 7) & 31, 0) * T, T)
            acc[to] += jnp.dot(vals[k], src[pl.ds(start, T), :], preferred_element_type=F32)


def first_body(ints, *refs):
    vals, pieces, acc, own_later, away_later = refs[0], refs[1:-6], refs[-6], refs[-5], refs[-4]
    src, now, piece_sem = refs[-3:]
    copies = []
    for i, (piece, row) in enumerate(zip(pieces, NEAR_ROWS)):
        copies.append(pltpu.make_async_copy(piece, src.at[pl.ds(row, piece.shape[0])], piece_sem.at[i]))
    for copy in copies:
        copy.start()

    @pl.loop(0, GRID + 1)
    def _(r):
        acc[r] = jnp.zeros((T, F), F32)

    used, here, core = ints[TILES], ints[TILES + 1], ints[TILES + 2]

    lists = (now, own_later, away_later)

    def sort(g, counts):
        for u in range(UNROLL):
            k = g * UNROLL + u
            at = ints[k]
            row, col = at >> 5, at & 31
            back = (here - (col >> 2)) & 7
            away = (row & 1) ^ core
            to = away * (GRID // 2) + (row >> 1)
            entry = k + (back * 4 + (col & 3)) * 128 + to * 4096
            for held, n in zip(lists, counts):
                held[n] = entry
            far = jnp.logical_and(back >= FAR_FROM, back < FAR_TO).astype(jnp.int32)
            live = (k < used).astype(jnp.int32)
            steps = (live * (1 - far), live * far * (1 - away), live * far * away)
            counts = tuple(n + step for n, step in zip(counts, steps))
        return counts

    counts = lax.fori_loop(0, (used + UNROLL - 1) // UNROLL, sort, (jnp.int32(0),) * 3)
    for held, n in zip(lists, counts):
        held[TILES + 1] = n
    for copy in copies:
        copy.wait()
    add_tiles(now, vals, src, acc, 0)


def first_sums(ints, tiles, pieces):
    smem = pl.BlockSpec(memory_space=pltpu.SMEM)
    vmem = pl.BlockSpec(memory_space=pltpu.VMEM)
    hbm = pl.BlockSpec(memory_space=pl.ANY)
    return pl.pallas_call(
        first_body,
        out_shape=(
            jax.ShapeDtypeStruct((GRID + 1, T, F), F32),
            jax.ShapeDtypeStruct((T,), jnp.int32),
            jax.ShapeDtypeStruct((T,), jnp.int32),
        ),
        in_specs=[smem, vmem] + [hbm] * len(pieces),
        out_specs=[vmem, smem, smem],
        scratch_shapes=[
            pltpu.VMEM((GRID * T, F), BF),
            pltpu.SMEM((T,), jnp.int32),
            pltpu.SemaphoreType.DMA((len(pieces),)),
        ],
        compiler_params=pltpu.CompilerParams(vmem_limit_bytes=24 * 2**20),
        cost_estimate=pl.CostEstimate(
            flops=2 * TILES * T * T * F, bytes_accessed=8 * 2**20, transcendentals=0
        ),
        name="first_sums",
    )(ints, tiles, *pieces)


def last_body(base, listed, begun, vals, *refs):
    pieces, out, src, acc, piece_sem = refs[:-4], refs[-4], refs[-3], refs[-2], refs[-1]
    copies = []
    for i, (piece, row) in enumerate(zip(pieces, FAR_ROWS)):
        copies.append(pltpu.make_async_copy(piece, src.at[pl.ds(row, piece.shape[0])], piece_sem.at[i]))
    for copy in copies:
        copy.start()

    @pl.loop(0, GRID // 2)
    def _(r):
        acc[r] = begun[base + r]

    for copy in copies:
        copy.wait()
    add_tiles(listed, vals, src, acc, base)

    @pl.loop(0, GRID // 2)
    def _(r):
        out[r] = acc[r].astype(out.dtype)


def last_sums(base, kind, listed, begun, vals, pieces):
    smem = pl.BlockSpec(memory_space=pltpu.SMEM)
    vmem = pl.BlockSpec(memory_space=pltpu.VMEM)
    hbm = pl.BlockSpec(memory_space=pl.ANY)
    return pl.pallas_call(
        functools.partial(last_body, base),
        out_shape=jax.ShapeDtypeStruct((GRID // 2, T, F), kind),
        in_specs=[smem, vmem, vmem] + [hbm] * len(pieces),
        out_specs=vmem,
        scratch_shapes=[
            pltpu.VMEM((GRID * T, F), BF),
            pltpu.VMEM((GRID // 2 + 1, T, F), F32),
            pltpu.SemaphoreType.DMA((len(pieces),)),
        ],
        compiler_params=pltpu.CompilerParams(vmem_limit_bytes=24 * 2**20),
        cost_estimate=pl.CostEstimate(
            flops=TILES * T * T * F, bytes_accessed=8 * 2**20, transcendentals=0
        ),
        name="last_away" if base else "last_own",
    )(listed, begun, vals, *pieces)


def finish_body(core, parts, order, weight, bias, out_grad, act_out, mine, other):
    total = parts[0].astype(F32)
    for i in range(1, parts.shape[0]):
        total += parts[i].astype(F32)
    agg = total.astype(BF)
    place = lax.broadcasted_iota(jnp.int32, (T, T), 0) == order[...]
    hot = place.astype(F32).astype(BF)
    pre = jnp.dot(agg, weight[...], preferred_element_type=F32) + bias[...]
    sig = jax.nn.sigmoid(pre)
    act = (pre * sig).astype(BF)
    act_out[...] = jnp.dot(hot, act, preferred_element_type=F32).astype(BF)
    cot = lax.dot_general(hot, out_grad[...], (((0,), (0,)), ((), ())), preferred_element_type=F32)
    grad = cot * sig * (1.0 + pre * (1.0 - sig))
    wgrad = lax.dot_general(
        agg, grad.astype(BF), (((0,), (0,)), ((), ())), preferred_element_type=F32
    )
    sums = jnp.sum(grad, axis=0, keepdims=True)
    first = core[0] == 0

    def halves(lead, low, high):
        return (jnp.where(lead, low, high), jnp.where(lead, high, low))

    own, away = halves(first, wgrad[:T], wgrad[T:])
    own_sum, away_sum = halves(first, sums[:, :T], sums[:, T:])
    for out, half, tail in ((mine, own, own_sum), (other, away, away_sum)):
        out[:, 0, 4 * F :] = jnp.zeros((GRID, T), F32)
        out[0:1, 0, 4 * F :] = tail
        for q in range(4):
            out[:, 0, q * F : (q + 1) * F] = half[q * GRID : (q + 1) * GRID]


def finish(core, parts, order, weight, bias, out_grad):
    smem = pl.BlockSpec(memory_space=pltpu.SMEM)
    vmem = pl.BlockSpec(memory_space=pltpu.VMEM)
    return pl.pallas_call(
        finish_body,
        out_shape=(
            jax.ShapeDtypeStruct((T, F), BF),
            jax.ShapeDtypeStruct((GRID, 1, 4 * F + T), F32),
            jax.ShapeDtypeStruct((GRID, 1, 4 * F + T), F32),
        ),
        in_specs=[smem] + [vmem] * 5,
        out_specs=[vmem] * 3,
        compiler_params=pltpu.CompilerParams(vmem_limit_bytes=40 * 2**20),
        name="finish",
    )(core, parts, order, weight, bias, out_grad)


def unpack_body(core, mine, other, wgrad, bgrad):
    first = core[0] == 0
    for c in range(2):
        pick = first if c == 0 else jnp.logical_not(first)
        for q in range(4):
            at = T * c + GRID * q
            lanes = slice(q * F, (q + 1) * F)
            wgrad[at : at + GRID, :] = jnp.where(pick, mine[:, 0, lanes], other[:, 0, lanes])
        bgrad[:, T * c : T * c + T] = jnp.where(pick, mine[0:1, 0, 4 * F :], other[0:1, 0, 4 * F :])


def unpack(core, mine, other):
    smem = pl.BlockSpec(memory_space=pltpu.SMEM)
    vmem = pl.BlockSpec(memory_space=pltpu.VMEM)
    return pl.pallas_call(
        unpack_body,
        out_shape=(jax.ShapeDtypeStruct((F, F), F32), jax.ShapeDtypeStruct((1, F), F32)),
        in_specs=[smem, vmem, vmem],
        out_specs=[vmem] * 2,
        compiler_params=pltpu.CompilerParams(vmem_limit_bytes=16 * 2**20),
        name="unpack",
    )(core, mine, other)


def ring_gather(own):
    def shift(block, by):
        return lax.ppermute(block, "y", [(i, (i + by) % 8) for i in range(8)])

    half = own.shape[0] // 2
    back1, ahead1, back2, ahead2 = (shift(own, by) for by in (1, -1, 2, -2))
    back3, ahead3 = shift(back2, 1), shift(ahead2, -1)
    far_low, far_high = shift(back2[:half], 2), shift(ahead2[half:], -2)
    return (own, back1, back2, ahead2, ahead1), (back3, far_low, far_high, ahead3)


def spread(block, axes, copies):
    repeated = jnp.broadcast_to(block[None], (copies, *block.shape))
    return lax.all_to_all(repeated, axes, 0, 0, tiled=True)


def local(features, node_order, tile_index, tile_count, tile_values, weight, out_bias, out_grad):
    swap = [(0, 1), (1, 0)]
    row_at = lax.axis_index("y").astype(jnp.int32)
    core = lax.axis_index("core").astype(jnp.int32)
    clustered = cluster(node_order, features)
    near = lax.all_gather(clustered, "zh", axis=0, tiled=True)
    early, late = ring_gather(near)
    ints = jnp.concatenate([tile_index[0], tile_count, jnp.stack([row_at, core])])
    vals = tile_values[0]
    begun, own_later, away_later = first_sums(ints, vals, early)
    away = lax.ppermute(last_sums(GRID // 2, BF, away_later, begun, vals, late), "core", swap)
    own = last_sums(0, F32, own_later, begun, vals, late)
    paired = (own + away.astype(F32)).astype(BF)
    parts = lax.all_to_all(paired, ("x", "zl"), 0, 0, tiled=True)
    core = core.reshape(1)
    activated, mine, other = finish(
        core, parts, node_order, weight, out_bias.reshape(1, F), out_grad
    )
    half = mine + lax.ppermute(other, "core", swap)
    block = lax.all_to_all(half, ("y", "x"), 0, 0, tiled=True).sum(axis=0)
    block = spread(block, ("zh", "zl"), 16).sum(axis=0)
    half = spread(block, ("y", "x"), GRID)
    weight_grad, bias_grad = unpack(core, half, lax.ppermute(half, "core", swap))
    return activated, weight_grad, bias_grad.reshape(F)


def solution(mesh):
    fine = Mesh(mesh.devices.reshape(8, 4, 4, 4, 2), AXES)
    return jax.shard_map(
        local,
        mesh=fine,
        in_specs=(
            P(AXES, None),
            P(AXES, None),
            P(AXES, None),
            P(AXES),
            P(AXES, None, None, None),
            P(),
            P(),
            P(AXES, None),
        ),
        out_specs=(P(AXES, None), P(), P()),
        check_vma=False,
    )
```

```python
import functools

import jax
import jax.numpy as jnp
from jax import lax
from jax.experimental import pallas as pl
from jax.experimental.pallas import tpu as pltpu
from jax.sharding import Mesh, PartitionSpec as P

AXES = ("y", "zh", "x", "zl", "core")
T = 128
F = 256
TILES = 96
GRID = 32
UNROLL = 8
FAR_FROM, FAR_TO = 3, 6
NEAR_ROWS = (0, 512, 1024, 3072, 3584)
FAR_ROWS = (1536, 2048, 2560)
BF = jnp.bfloat16
F32 = jnp.float32


def cluster_body(order, feats, out):
    place = lax.broadcasted_iota(jnp.int32, (T, T), 0) == order[...]
    hot = place.astype(F32).astype(BF)
    out[...] = lax.dot_general(
        hot, feats[...], (((0,), (0,)), ((), ())), preferred_element_type=F32
    ).astype(BF)


def cluster(order, feats):
    return pl.pallas_call(
        cluster_body,
        out_shape=jax.ShapeDtypeStruct((T, F), BF),
        name="cluster",
    )(order, feats)


def add_tiles(listed, vals, src, acc, base):
    used, spare = listed[TILES + 1], acc.shape[0] - 1

    @pl.loop(0, (used + UNROLL - 1) // UNROLL)
    def _(g):
        for u in range(UNROLL):
            i = g * UNROLL + u
            entry = listed[i]
            to = jnp.where(i < used, (entry >> 12) - base, spare)
            k = jnp.where(i < used, entry & 127, 0)
            start = pl.multiple_of(jnp.where(i < used, (entry >> 7) & 31, 0) * T, T)
            acc[to] += jnp.dot(vals[k], src[pl.ds(start, T), :], preferred_element_type=F32)


def first_body(ints, *refs):
    vals, pieces, acc, own_later, away_later = refs[0], refs[1:-6], refs[-6], refs[-5], refs[-4]
    src, now, piece_sem = refs[-3:]
    copies = []
    for i, (piece, row) in enumerate(zip(pieces, NEAR_ROWS)):
        copies.append(pltpu.make_async_copy(piece, src.at[pl.ds(row, piece.shape[0])], piece_sem.at[i]))
    for copy in copies:
        copy.start()

    @pl.loop(0, GRID + 1)
    def _(r):
        acc[r] = jnp.zeros((T, F), F32)

    used, here, core = ints[TILES], ints[TILES + 1], ints[TILES + 2]

    lists = (now, own_later, away_later)

    def sort(g, counts):
        for u in range(UNROLL):
            k = g * UNROLL + u
            at = ints[k]
            row, col = at >> 5, at & 31
            back = (here - (col >> 2)) & 7
            away = (row & 1) ^ core
            to = away * (GRID // 2) + (row >> 1)
            entry = k + (back * 4 + (col & 3)) * 128 + to * 4096
            for held, n in zip(lists, counts):
                held[n] = entry
            far = jnp.logical_and(back >= FAR_FROM, back < FAR_TO).astype(jnp.int32)
            live = (k < used).astype(jnp.int32)
            steps = (live * (1 - far), live * far * (1 - away), live * far * away)
            counts = tuple(n + step for n, step in zip(counts, steps))
        return counts

    counts = lax.fori_loop(0, (used + UNROLL - 1) // UNROLL, sort, (jnp.int32(0),) * 3)
    for held, n in zip(lists, counts):
        held[TILES + 1] = n
    for copy in copies:
        copy.wait()
    add_tiles(now, vals, src, acc, 0)


def first_sums(ints, tiles, pieces):
    smem = pl.BlockSpec(memory_space=pltpu.SMEM)
    vmem = pl.BlockSpec(memory_space=pltpu.VMEM)
    hbm = pl.BlockSpec(memory_space=pl.ANY)
    return pl.pallas_call(
        first_body,
        out_shape=(
            jax.ShapeDtypeStruct((GRID + 1, T, F), F32),
            jax.ShapeDtypeStruct((T,), jnp.int32),
            jax.ShapeDtypeStruct((T,), jnp.int32),
        ),
        in_specs=[smem, vmem] + [hbm] * len(pieces),
        out_specs=[vmem, smem, smem],
        scratch_shapes=[
            pltpu.VMEM((GRID * T, F), BF),
            pltpu.SMEM((T,), jnp.int32),
            pltpu.SemaphoreType.DMA((len(pieces),)),
        ],
        compiler_params=pltpu.CompilerParams(vmem_limit_bytes=24 * 2**20),
        cost_estimate=pl.CostEstimate(
            flops=2 * TILES * T * T * F, bytes_accessed=8 * 2**20, transcendentals=0
        ),
        name="first_sums",
    )(ints, tiles, *pieces)


def last_body(base, listed, begun, vals, *refs):
    pieces, out, src, acc, piece_sem = refs[:-4], refs[-4], refs[-3], refs[-2], refs[-1]
    copies = []
    for i, (piece, row) in enumerate(zip(pieces, FAR_ROWS)):
        copies.append(pltpu.make_async_copy(piece, src.at[pl.ds(row, piece.shape[0])], piece_sem.at[i]))
    for copy in copies:
        copy.start()

    @pl.loop(0, GRID // 2)
    def _(r):
        acc[r] = begun[base + r]

    for copy in copies:
        copy.wait()
    add_tiles(listed, vals, src, acc, base)

    @pl.loop(0, GRID // 2)
    def _(r):
        out[r] = acc[r].astype(out.dtype)


def last_sums(base, kind, listed, begun, vals, pieces):
    smem = pl.BlockSpec(memory_space=pltpu.SMEM)
    vmem = pl.BlockSpec(memory_space=pltpu.VMEM)
    hbm = pl.BlockSpec(memory_space=pl.ANY)
    return pl.pallas_call(
        functools.partial(last_body, base),
        out_shape=jax.ShapeDtypeStruct((GRID // 2, T, F), kind),
        in_specs=[smem, vmem, vmem] + [hbm] * len(pieces),
        out_specs=vmem,
        scratch_shapes=[
            pltpu.VMEM((GRID * T, F), BF),
            pltpu.VMEM((GRID // 2 + 1, T, F), F32),
            pltpu.SemaphoreType.DMA((len(pieces),)),
        ],
        compiler_params=pltpu.CompilerParams(vmem_limit_bytes=24 * 2**20),
        cost_estimate=pl.CostEstimate(
            flops=TILES * T * T * F, bytes_accessed=8 * 2**20, transcendentals=0
        ),
        name="last_away" if base else "last_own",
    )(listed, begun, vals, *pieces)


def finish_body(core, parts, order, weight, bias, out_grad, act_out, mine, other):
    total = parts[0].astype(F32)
    for i in range(1, parts.shape[0]):
        total += parts[i].astype(F32)
    agg = total.astype(BF)
    place = lax.broadcasted_iota(jnp.int32, (T, T), 0) == order[...]
    hot = place.astype(F32).astype(BF)
    pre = jnp.dot(agg, weight[...], preferred_element_type=F32) + bias[...]
    sig = jax.nn.sigmoid(pre)
    act = (pre * sig).astype(BF)
    act_out[...] = jnp.dot(hot, act, preferred_element_type=F32).astype(BF)
    cot = lax.dot_general(hot, out_grad[...], (((0,), (0,)), ((), ())), preferred_element_type=F32)
    grad = cot * sig * (1.0 + pre * (1.0 - sig))
    wgrad = lax.dot_general(
        agg, grad.astype(BF), (((0,), (0,)), ((), ())), preferred_element_type=F32
    )
    sums = jnp.sum(grad, axis=0, keepdims=True)
    first = core[0] == 0

    def halves(lead, low, high):
        return (jnp.where(lead, low, high), jnp.where(lead, high, low))

    own, away = halves(first, wgrad[:T], wgrad[T:])
    own_sum, away_sum = halves(first, sums[:, :T], sums[:, T:])
    for out, half, tail in ((mine, own, own_sum), (other, away, away_sum)):
        out[:, 0, 4 * F :] = jnp.zeros((GRID, T), F32)
        out[0:1, 0, 4 * F :] = tail
        for q in range(4):
            out[:, 0, q * F : (q + 1) * F] = half[q * GRID : (q + 1) * GRID]


def finish(core, parts, order, weight, bias, out_grad):
    smem = pl.BlockSpec(memory_space=pltpu.SMEM)
    vmem = pl.BlockSpec(memory_space=pltpu.VMEM)
    return pl.pallas_call(
        finish_body,
        out_shape=(
            jax.ShapeDtypeStruct((T, F), BF),
            jax.ShapeDtypeStruct((GRID, 1, 4 * F + T), F32),
            jax.ShapeDtypeStruct((GRID, 1, 4 * F + T), F32),
        ),
        in_specs=[smem] + [vmem] * 5,
        out_specs=[vmem] * 3,
        compiler_params=pltpu.CompilerParams(vmem_limit_bytes=40 * 2**20),
        name="finish",
    )(core, parts, order, weight, bias, out_grad)


def unpack_body(core, mine, other, wgrad, bgrad):
    first = core[0] == 0
    for c in range(2):
        pick = first if c == 0 else jnp.logical_not(first)
        for q in range(4):
            at = T * c + GRID * q
            lanes = slice(q * F, (q + 1) * F)
            wgrad[at : at + GRID, :] = jnp.where(pick, mine[:, 0, lanes], other[:, 0, lanes])
        bgrad[:, T * c : T * c + T] = jnp.where(pick, mine[0:1, 0, 4 * F :], other[0:1, 0, 4 * F :])


def unpack(core, mine, other):
    smem = pl.BlockSpec(memory_space=pltpu.SMEM)
    vmem = pl.BlockSpec(memory_space=pltpu.VMEM)
    return pl.pallas_call(
        unpack_body,
        out_shape=(jax.ShapeDtypeStruct((F, F), F32), jax.ShapeDtypeStruct((1, F), F32)),
        in_specs=[smem, vmem, vmem],
        out_specs=[vmem] * 2,
        compiler_params=pltpu.CompilerParams(vmem_limit_bytes=16 * 2**20),
        name="unpack",
    )(core, mine, other)


def ring_gather(own, core):
    def shift(block, by):
        return lax.ppermute(block, "y", [(i, (i + by) % 8) for i in range(8)])

    back1, ahead1, back2, ahead2 = (shift(own, by) for by in (1, -1, 2, -2))
    back3, ahead3 = shift(back2, 1), shift(ahead2, -1)
    hops = [(2 * i + c, 2 * ((i + (2, -2)[c]) % 8) + c) for i in range(8) for c in range(2)]
    far = lax.ppermute(jnp.where(core == 0, back2, ahead2), ("y", "core"), hops)
    return (own, back1, back2, ahead2, ahead1), (back3, far, ahead3)


def spread(block, axes, copies):
    repeated = jnp.broadcast_to(block[None], (copies, *block.shape))
    return lax.all_to_all(repeated, axes, 0, 0, tiled=True)


def local(features, node_order, tile_index, tile_count, tile_values, weight, out_bias, out_grad):
    swap = [(0, 1), (1, 0)]
    row_at = lax.axis_index("y").astype(jnp.int32)
    core = lax.axis_index("core").astype(jnp.int32)
    clustered = cluster(node_order, features)
    near = lax.all_gather(clustered, "zh", axis=0, tiled=True)
    early, late = ring_gather(near, core)
    ints = jnp.concatenate([tile_index[0], tile_count, jnp.stack([row_at, core])])
    vals = tile_values[0]
    begun, own_later, away_later = first_sums(ints, vals, early)
    away = lax.ppermute(last_sums(GRID // 2, BF, away_later, begun, vals, late), "core", swap)
    own = last_sums(0, F32, own_later, begun, vals, late)
    paired = (own + away.astype(F32)).astype(BF)
    parts = lax.all_to_all(paired, ("x", "zl"), 0, 0, tiled=True)
    core = core.reshape(1)
    activated, mine, other = finish(
        core, parts, node_order, weight, out_bias.reshape(1, F), out_grad
    )
    half = mine + lax.ppermute(other, "core", swap)
    block = lax.all_to_all(half, ("y", "x"), 0, 0, tiled=True).sum(axis=0)
    block = spread(block, ("zh", "zl"), 16).sum(axis=0)
    half = spread(block, ("y", "x"), GRID)
    weight_grad, bias_grad = unpack(core, half, lax.ppermute(half, "core", swap))
    return activated, weight_grad, bias_grad.reshape(F)


def solution(mesh):
    fine = Mesh(mesh.devices.reshape(8, 4, 4, 4, 2), AXES)
    return jax.shard_map(
        local,
        mesh=fine,
        in_specs=(
            P(AXES, None),
            P(AXES, None),
            P(AXES, None),
            P(AXES),
            P(AXES, None, None, None),
            P(),
            P(),
            P(AXES, None),
        ),
        out_specs=(P(AXES, None), P(), P()),
        check_vma=False,
    )
```

```python
import functools

import jax
import jax.numpy as jnp
from jax import lax
from jax.experimental import pallas as pl
from jax.experimental.pallas import tpu as pltpu
from jax.sharding import Mesh, PartitionSpec as P

AXES = ("y", "zh", "x", "zl", "core")
T = 128
F = 256
TILES = 96
GRID = 32
UNROLL = 8
FAR_FROM, FAR_TO = 3, 6
NEAR_ROWS = (0, 512, 1024, 3072, 3584)
FAR_ROWS = (1536, 2048, 2560)
BF = jnp.bfloat16
F32 = jnp.float32


def cluster_body(order, feats, out):
    place = lax.broadcasted_iota(jnp.int32, (T, T), 0) == order[...]
    hot = place.astype(F32).astype(BF)
    out[...] = lax.dot_general(
        hot, feats[...], (((0,), (0,)), ((), ())), preferred_element_type=F32
    ).astype(BF)


def cluster(order, feats):
    return pl.pallas_call(
        cluster_body,
        out_shape=jax.ShapeDtypeStruct((T, F), BF),
        name="cluster",
    )(order, feats)


def add_tiles(listed, vals, src, acc, base):
    used, spare = listed[TILES + 1], acc.shape[0] - 1

    @pl.loop(0, (used + UNROLL - 1) // UNROLL)
    def _(g):
        for u in range(UNROLL):
            i = g * UNROLL + u
            entry = listed[i]
            to = jnp.where(i < used, (entry >> 12) - base, spare)
            k = jnp.where(i < used, entry & 127, 0)
            start = pl.multiple_of(jnp.where(i < used, (entry >> 7) & 31, 0) * T, T)
            acc[to] += jnp.dot(vals[k], src[pl.ds(start, T), :], preferred_element_type=F32)


def first_body(ints, *refs):
    vals, pieces, acc, own_later, away_later = refs[0], refs[1:-6], refs[-6], refs[-5], refs[-4]
    src, now, piece_sem = refs[-3:]
    copies = []
    for i, (piece, row) in enumerate(zip(pieces, NEAR_ROWS)):
        copies.append(pltpu.make_async_copy(piece, src.at[pl.ds(row, piece.shape[0])], piece_sem.at[i]))
    for copy in copies:
        copy.start()

    @pl.loop(0, GRID + 1)
    def _(r):
        acc[r] = jnp.zeros((T, F), F32)

    used, here, core = ints[TILES], ints[TILES + 1], ints[TILES + 2]

    lists = (now, own_later, away_later)

    def sort(g, counts):
        for u in range(UNROLL):
            k = g * UNROLL + u
            at = ints[k]
            row, col = at >> 5, at & 31
            back = (here - (col >> 2)) & 7
            away = (row & 1) ^ core
            to = away * (GRID // 2) + (row >> 1)
            entry = k + (back * 4 + (col & 3)) * 128 + to * 4096
            for held, n in zip(lists, counts):
                held[n] = entry
            far = jnp.logical_and(back >= FAR_FROM, back < FAR_TO).astype(jnp.int32)
            live = (k < used).astype(jnp.int32)
            steps = (live * (1 - far), live * far * (1 - away), live * far * away)
            counts = tuple(n + step for n, step in zip(counts, steps))
        return counts

    counts = lax.fori_loop(0, (used + UNROLL - 1) // UNROLL, sort, (jnp.int32(0),) * 3)
    for held, n in zip(lists, counts):
        held[TILES + 1] = n
    for copy in copies:
        copy.wait()
    add_tiles(now, vals, src, acc, 0)


def first_sums(ints, tiles, pieces):
    smem = pl.BlockSpec(memory_space=pltpu.SMEM)
    vmem = pl.BlockSpec(memory_space=pltpu.VMEM)
    hbm = pl.BlockSpec(memory_space=pl.ANY)
    return pl.pallas_call(
        first_body,
        out_shape=(
            jax.ShapeDtypeStruct((GRID + 1, T, F), F32),
            jax.ShapeDtypeStruct((T,), jnp.int32),
            jax.ShapeDtypeStruct((T,), jnp.int32),
        ),
        in_specs=[smem, vmem] + [hbm] * len(pieces),
        out_specs=[vmem, smem, smem],
        scratch_shapes=[
            pltpu.VMEM((GRID * T, F), BF),
            pltpu.SMEM((T,), jnp.int32),
            pltpu.SemaphoreType.DMA((len(pieces),)),
        ],
        compiler_params=pltpu.CompilerParams(vmem_limit_bytes=24 * 2**20),
        cost_estimate=pl.CostEstimate(
            flops=2 * TILES * T * T * F, bytes_accessed=8 * 2**20, transcendentals=0
        ),
        name="first_sums",
    )(ints, tiles, *pieces)


def last_body(base, listed, begun, vals, *refs):
    pieces, out, src, acc, piece_sem = refs[:-4], refs[-4], refs[-3], refs[-2], refs[-1]
    copies = []
    for i, (piece, row) in enumerate(zip(pieces, FAR_ROWS)):
        copies.append(pltpu.make_async_copy(piece, src.at[pl.ds(row, piece.shape[0])], piece_sem.at[i]))
    for copy in copies:
        copy.start()

    @pl.loop(0, GRID // 2)
    def _(r):
        acc[r] = begun[base + r]

    for copy in copies:
        copy.wait()
    add_tiles(listed, vals, src, acc, base)

    @pl.loop(0, GRID // 2)
    def _(r):
        out[r] = acc[r].astype(out.dtype)


def last_sums(base, kind, listed, begun, vals, pieces):
    smem = pl.BlockSpec(memory_space=pltpu.SMEM)
    vmem = pl.BlockSpec(memory_space=pltpu.VMEM)
    hbm = pl.BlockSpec(memory_space=pl.ANY)
    return pl.pallas_call(
        functools.partial(last_body, base),
        out_shape=jax.ShapeDtypeStruct((GRID // 2, T, F), kind),
        in_specs=[smem, vmem, vmem] + [hbm] * len(pieces),
        out_specs=vmem,
        scratch_shapes=[
            pltpu.VMEM((GRID * T, F), BF),
            pltpu.VMEM((GRID // 2 + 1, T, F), F32),
            pltpu.SemaphoreType.DMA((len(pieces),)),
        ],
        compiler_params=pltpu.CompilerParams(vmem_limit_bytes=24 * 2**20),
        cost_estimate=pl.CostEstimate(
            flops=TILES * T * T * F, bytes_accessed=8 * 2**20, transcendentals=0
        ),
        name="last_away" if base else "last_own",
    )(listed, begun, vals, *pieces)


def finish_body(core, parts, order, weight, bias, out_grad, act_out, mine, other):
    total = parts[0].astype(F32)
    for i in range(1, parts.shape[0]):
        total += parts[i].astype(F32)
    agg = total.astype(BF)
    place = lax.broadcasted_iota(jnp.int32, (T, T), 0) == order[...]
    hot = place.astype(F32).astype(BF)
    pre = jnp.dot(agg, weight[...], preferred_element_type=F32) + bias[...]
    sig = jax.nn.sigmoid(pre)
    act = (pre * sig).astype(BF)
    act_out[...] = jnp.dot(hot, act, preferred_element_type=F32).astype(BF)
    cot = lax.dot_general(hot, out_grad[...], (((0,), (0,)), ((), ())), preferred_element_type=F32)
    grad = cot * sig * (1.0 + pre * (1.0 - sig))
    wgrad = lax.dot_general(
        agg, grad.astype(BF), (((0,), (0,)), ((), ())), preferred_element_type=F32
    )
    sums = jnp.sum(grad, axis=0, keepdims=True)
    first = core[0] == 0

    def halves(lead, low, high):
        return (jnp.where(lead, low, high), jnp.where(lead, high, low))

    own, away = halves(first, wgrad[:T], wgrad[T:])
    own_sum, away_sum = halves(first, sums[:, :T], sums[:, T:])
    for out, half, tail in ((mine, own, own_sum), (other, away, away_sum)):
        out[:, 0, 4 * F :] = jnp.zeros((GRID, T), F32)
        out[0:1, 0, 4 * F :] = tail
        for q in range(4):
            out[:, 0, q * F : (q + 1) * F] = half[q * GRID : (q + 1) * GRID]


def finish(core, parts, order, weight, bias, out_grad):
    smem = pl.BlockSpec(memory_space=pltpu.SMEM)
    vmem = pl.BlockSpec(memory_space=pltpu.VMEM)
    return pl.pallas_call(
        finish_body,
        out_shape=(
            jax.ShapeDtypeStruct((T, F), BF),
            jax.ShapeDtypeStruct((GRID, 1, 4 * F + T), F32),
            jax.ShapeDtypeStruct((GRID, 1, 4 * F + T), F32),
        ),
        in_specs=[smem] + [vmem] * 5,
        out_specs=[vmem] * 3,
        compiler_params=pltpu.CompilerParams(vmem_limit_bytes=40 * 2**20),
        name="finish",
    )(core, parts, order, weight, bias, out_grad)


def unpack_body(core, mine, other, wgrad, bgrad):
    first = core[0] == 0
    for c in range(2):
        pick = first if c == 0 else jnp.logical_not(first)
        for q in range(4):
            at = T * c + GRID * q
            lanes = slice(q * F, (q + 1) * F)
            wgrad[at : at + GRID, :] = jnp.where(pick, mine[:, 0, lanes], other[:, 0, lanes])
        bgrad[:, T * c : T * c + T] = jnp.where(pick, mine[0:1, 0, 4 * F :], other[0:1, 0, 4 * F :])


def unpack(core, mine, other):
    smem = pl.BlockSpec(memory_space=pltpu.SMEM)
    vmem = pl.BlockSpec(memory_space=pltpu.VMEM)
    return pl.pallas_call(
        unpack_body,
        out_shape=(jax.ShapeDtypeStruct((F, F), F32), jax.ShapeDtypeStruct((1, F), F32)),
        in_specs=[smem, vmem, vmem],
        out_specs=[vmem] * 2,
        compiler_params=pltpu.CompilerParams(vmem_limit_bytes=16 * 2**20),
        name="unpack",
    )(core, mine, other)


def ring_gather(own, core):
    def shift(block, by):
        return lax.ppermute(block, "y", [(i, (i + by) % 8) for i in range(8)])

    back1, ahead1, back2, ahead2 = (shift(own, by) for by in (1, -1, 2, -2))
    back3, ahead3 = shift(back2, 1), shift(ahead2, -1)
    hops = [(2 * i + c, 2 * ((i + (-2, 2)[c]) % 8) + c) for i in range(8) for c in range(2)]
    far = lax.ppermute(jnp.where(core == 0, ahead2, back2), ("y", "core"), hops)
    return (own, back1, back2, ahead2, ahead1), (back3, far, ahead3)


def spread(block, axes, copies):
    repeated = jnp.broadcast_to(block[None], (copies, *block.shape))
    return lax.all_to_all(repeated, axes, 0, 0, tiled=True)


def local(features, node_order, tile_index, tile_count, tile_values, weight, out_bias, out_grad):
    swap = [(0, 1), (1, 0)]
    row_at = lax.axis_index("y").astype(jnp.int32)
    core = lax.axis_index("core").astype(jnp.int32)
    clustered = cluster(node_order, features)
    near = lax.all_gather(clustered, "zh", axis=0, tiled=True)
    early, late = ring_gather(near, core)
    ints = jnp.concatenate([tile_index[0], tile_count, jnp.stack([row_at, core])])
    vals = tile_values[0]
    begun, own_later, away_later = first_sums(ints, vals, early)
    away = lax.ppermute(last_sums(GRID // 2, BF, away_later, begun, vals, late), "core", swap)
    own = last_sums(0, F32, own_later, begun, vals, late)
    paired = (own + away.astype(F32)).astype(BF)
    parts = lax.all_to_all(paired, ("x", "zl"), 0, 0, tiled=True)
    core = core.reshape(1)
    activated, mine, other = finish(
        core, parts, node_order, weight, out_bias.reshape(1, F), out_grad
    )
    half = mine + lax.ppermute(other, "core", swap)
    block = lax.all_to_all(half, ("y", "x"), 0, 0, tiled=True).sum(axis=0)
    block = spread(block, ("zh", "zl"), 16).sum(axis=0)
    half = spread(block, ("y", "x"), GRID)
    weight_grad, bias_grad = unpack(core, half, lax.ppermute(half, "core", swap))
    return activated, weight_grad, bias_grad.reshape(F)


def solution(mesh):
    fine = Mesh(mesh.devices.reshape(8, 4, 4, 4, 2), AXES)
    return jax.shard_map(
        local,
        mesh=fine,
        in_specs=(
            P(AXES, None),
            P(AXES, None),
            P(AXES, None),
            P(AXES),
            P(AXES, None, None, None),
            P(),
            P(),
            P(AXES, None),
        ),
        out_specs=(P(AXES, None), P(), P()),
        check_vma=False,
    )
```

```python
import functools

import jax
import jax.numpy as jnp
from jax import lax
from jax.experimental import pallas as pl
from jax.experimental.pallas import tpu as pltpu
from jax.sharding import Mesh, PartitionSpec as P

AXES = ("y", "zh", "x", "zl", "core")
T = 128
F = 256
TILES = 96
GRID = 32
UNROLL = 8
FAR_FROM, FAR_TO = 3, 6
NEAR_ROWS = (0, 512, 1024, 3072, 3584)
FAR_ROWS = (1536, 2048, 2560)
BF = jnp.bfloat16
F32 = jnp.float32


def cluster_body(order, feats, out):
    place = lax.broadcasted_iota(jnp.int32, (T, T), 0) == order[...]
    hot = place.astype(F32).astype(BF)
    out[...] = lax.dot_general(
        hot, feats[...], (((0,), (0,)), ((), ())), preferred_element_type=F32
    ).astype(BF)


def cluster(order, feats):
    return pl.pallas_call(
        cluster_body,
        out_shape=jax.ShapeDtypeStruct((T, F), BF),
        name="cluster",
    )(order, feats)


def add_tiles(listed, vals, src, acc, base):
    used, spare = listed[TILES + 1], acc.shape[0] - 1

    @pl.loop(0, (used + UNROLL - 1) // UNROLL)
    def _(g):
        for u in range(UNROLL):
            i = g * UNROLL + u
            entry = listed[i]
            to = jnp.where(i < used, (entry >> 12) - base, spare)
            k = jnp.where(i < used, entry & 127, 0)
            start = pl.multiple_of(jnp.where(i < used, (entry >> 7) & 31, 0) * T, T)
            acc[to] += jnp.dot(vals[k], src[pl.ds(start, T), :], preferred_element_type=F32)


def first_body(ints, *refs):
    vals, pieces, acc, own_later, away_later = refs[0], refs[1:-6], refs[-6], refs[-5], refs[-4]
    src, now, piece_sem = refs[-3:]
    copies = []
    for i, (piece, row) in enumerate(zip(pieces, NEAR_ROWS)):
        copies.append(pltpu.make_async_copy(piece, src.at[pl.ds(row, piece.shape[0])], piece_sem.at[i]))
    for copy in copies:
        copy.start()

    @pl.loop(0, GRID + 1)
    def _(r):
        acc[r] = jnp.zeros((T, F), F32)

    used, here, core = ints[TILES], ints[TILES + 1], ints[TILES + 2]

    lists = (now, own_later, away_later)

    def sort(g, counts):
        for u in range(UNROLL):
            k = g * UNROLL + u
            at = ints[k]
            row, col = at >> 5, at & 31
            back = (here - (col >> 2)) & 7
            away = (row & 1) ^ core
            to = away * (GRID // 2) + ((row >> 1) & 3) * 4 + (row >> 3)
            entry = k + (back * 4 + (col & 3)) * 128 + to * 4096
            for held, n in zip(lists, counts):
                held[n] = entry
            far = jnp.logical_and(back >= FAR_FROM, back < FAR_TO).astype(jnp.int32)
            live = (k < used).astype(jnp.int32)
            steps = (live * (1 - far), live * far * (1 - away), live * far * away)
            counts = tuple(n + step for n, step in zip(counts, steps))
        return counts

    counts = lax.fori_loop(0, (used + UNROLL - 1) // UNROLL, sort, (jnp.int32(0),) * 3)
    for held, n in zip(lists, counts):
        held[TILES + 1] = n
    for copy in copies:
        copy.wait()
    add_tiles(now, vals, src, acc, 0)


def first_sums(ints, tiles, pieces):
    smem = pl.BlockSpec(memory_space=pltpu.SMEM)
    vmem = pl.BlockSpec(memory_space=pltpu.VMEM)
    hbm = pl.BlockSpec(memory_space=pl.ANY)
    return pl.pallas_call(
        first_body,
        out_shape=(
            jax.ShapeDtypeStruct((GRID + 1, T, F), F32),
            jax.ShapeDtypeStruct((T,), jnp.int32),
            jax.ShapeDtypeStruct((T,), jnp.int32),
        ),
        in_specs=[smem, vmem] + [hbm] * len(pieces),
        out_specs=[vmem, smem, smem],
        scratch_shapes=[
            pltpu.VMEM((GRID * T, F), BF),
            pltpu.SMEM((T,), jnp.int32),
            pltpu.SemaphoreType.DMA((len(pieces),)),
        ],
        compiler_params=pltpu.CompilerParams(vmem_limit_bytes=24 * 2**20),
        cost_estimate=pl.CostEstimate(
            flops=2 * TILES * T * T * F, bytes_accessed=8 * 2**20, transcendentals=0
        ),
        name="first_sums",
    )(ints, tiles, *pieces)


def last_body(base, listed, begun, vals, *refs):
    pieces, out, src, acc, piece_sem = refs[:-4], refs[-4], refs[-3], refs[-2], refs[-1]
    copies = []
    for i, (piece, row) in enumerate(zip(pieces, FAR_ROWS)):
        copies.append(pltpu.make_async_copy(piece, src.at[pl.ds(row, piece.shape[0])], piece_sem.at[i]))
    for copy in copies:
        copy.start()

    @pl.loop(0, GRID // 2)
    def _(r):
        acc[r] = begun[base + r]

    for copy in copies:
        copy.wait()
    add_tiles(listed, vals, src, acc, base)

    @pl.loop(0, GRID // 2)
    def _(r):
        out[r] = acc[r].astype(out.dtype)


def last_sums(base, kind, listed, begun, vals, pieces):
    smem = pl.BlockSpec(memory_space=pltpu.SMEM)
    vmem = pl.BlockSpec(memory_space=pltpu.VMEM)
    hbm = pl.BlockSpec(memory_space=pl.ANY)
    return pl.pallas_call(
        functools.partial(last_body, base),
        out_shape=jax.ShapeDtypeStruct((GRID // 2, T, F), kind),
        in_specs=[smem, vmem, vmem] + [hbm] * len(pieces),
        out_specs=vmem,
        scratch_shapes=[
            pltpu.VMEM((GRID * T, F), BF),
            pltpu.VMEM((GRID // 2 + 1, T, F), F32),
            pltpu.SemaphoreType.DMA((len(pieces),)),
        ],
        compiler_params=pltpu.CompilerParams(vmem_limit_bytes=24 * 2**20),
        cost_estimate=pl.CostEstimate(
            flops=TILES * T * T * F, bytes_accessed=8 * 2**20, transcendentals=0
        ),
        name="last_away" if base else "last_own",
    )(listed, begun, vals, *pieces)


def finish_body(core, parts, order, weight, bias, out_grad, act_out, mine, other):
    total = parts[0].astype(F32)
    for i in range(1, parts.shape[0]):
        total += parts[i].astype(F32)
    agg = total.astype(BF)
    place = lax.broadcasted_iota(jnp.int32, (T, T), 0) == order[...]
    hot = place.astype(F32).astype(BF)
    pre = jnp.dot(agg, weight[...], preferred_element_type=F32) + bias[...]
    sig = jax.nn.sigmoid(pre)
    act = (pre * sig).astype(BF)
    act_out[...] = jnp.dot(hot, act, preferred_element_type=F32).astype(BF)
    cot = lax.dot_general(hot, out_grad[...], (((0,), (0,)), ((), ())), preferred_element_type=F32)
    grad = cot * sig * (1.0 + pre * (1.0 - sig))
    wgrad = lax.dot_general(
        agg, grad.astype(BF), (((0,), (0,)), ((), ())), preferred_element_type=F32
    )
    sums = jnp.sum(grad, axis=0, keepdims=True)
    first = core[0] == 0

    def halves(lead, low, high):
        return (jnp.where(lead, low, high), jnp.where(lead, high, low))

    own, away = halves(first, wgrad[:T], wgrad[T:])
    own_sum, away_sum = halves(first, sums[:, :T], sums[:, T:])
    for out, half, tail in ((mine, own, own_sum), (other, away, away_sum)):
        out[:, 0, 4 * F :] = jnp.zeros((GRID, T), F32)
        out[0:1, 0, 4 * F :] = tail
        for q in range(4):
            out[:, 0, q * F : (q + 1) * F] = half[q * GRID : (q + 1) * GRID]


def finish(core, parts, order, weight, bias, out_grad):
    smem = pl.BlockSpec(memory_space=pltpu.SMEM)
    vmem = pl.BlockSpec(memory_space=pltpu.VMEM)
    return pl.pallas_call(
        finish_body,
        out_shape=(
            jax.ShapeDtypeStruct((T, F), BF),
            jax.ShapeDtypeStruct((GRID, 1, 4 * F + T), F32),
            jax.ShapeDtypeStruct((GRID, 1, 4 * F + T), F32),
        ),
        in_specs=[smem] + [vmem] * 5,
        out_specs=[vmem] * 3,
        compiler_params=pltpu.CompilerParams(vmem_limit_bytes=40 * 2**20),
        name="finish",
    )(core, parts, order, weight, bias, out_grad)


def unpack_body(core, mine, other, wgrad, bgrad):
    first = core[0] == 0
    for c in range(2):
        pick = first if c == 0 else jnp.logical_not(first)
        for q in range(4):
            at = T * c + GRID * q
            lanes = slice(q * F, (q + 1) * F)
            wgrad[at : at + GRID, :] = jnp.where(pick, mine[:, 0, lanes], other[:, 0, lanes])
        bgrad[:, T * c : T * c + T] = jnp.where(pick, mine[0:1, 0, 4 * F :], other[0:1, 0, 4 * F :])


def unpack(core, mine, other):
    smem = pl.BlockSpec(memory_space=pltpu.SMEM)
    vmem = pl.BlockSpec(memory_space=pltpu.VMEM)
    return pl.pallas_call(
        unpack_body,
        out_shape=(jax.ShapeDtypeStruct((F, F), F32), jax.ShapeDtypeStruct((1, F), F32)),
        in_specs=[smem, vmem, vmem],
        out_specs=[vmem] * 2,
        compiler_params=pltpu.CompilerParams(vmem_limit_bytes=16 * 2**20),
        name="unpack",
    )(core, mine, other)


def ring_gather(own, core):
    def shift(block, by):
        return lax.ppermute(block, "y", [(i, (i + by) % 8) for i in range(8)])

    back1, ahead1, back2, ahead2 = (shift(own, by) for by in (1, -1, 2, -2))
    back3, ahead3 = shift(back2, 1), shift(ahead2, -1)
    hops = [(2 * i + c, 2 * ((i + (-2, 2)[c]) % 8) + c) for i in range(8) for c in range(2)]
    far = lax.ppermute(jnp.where(core == 0, ahead2, back2), ("y", "core"), hops)
    return (own, back1, back2, ahead2, ahead1), (back3, far, ahead3)


def spread(block, axes, copies):
    repeated = jnp.broadcast_to(block[None], (copies, *block.shape))
    return lax.all_to_all(repeated, axes, 0, 0, tiled=True)


def local(features, node_order, tile_index, tile_count, tile_values, weight, out_bias, out_grad):
    swap = [(0, 1), (1, 0)]
    row_at = lax.axis_index("y").astype(jnp.int32)
    core = lax.axis_index("core").astype(jnp.int32)
    clustered = cluster(node_order, features)
    near = lax.all_gather(clustered, "zh", axis=0, tiled=True)
    early, late = ring_gather(near, core)
    ints = jnp.concatenate([tile_index[0], tile_count, jnp.stack([row_at, core])])
    vals = tile_values[0]
    begun, own_later, away_later = first_sums(ints, vals, early)
    away = lax.ppermute(last_sums(GRID // 2, BF, away_later, begun, vals, late), "core", swap)
    own = last_sums(0, F32, own_later, begun, vals, late)
    paired = (own + away.astype(F32)).astype(BF)
    parts = lax.all_to_all(paired, ("zl", "x"), 0, 0, tiled=True)
    core = core.reshape(1)
    activated, mine, other = finish(
        core, parts, node_order, weight, out_bias.reshape(1, F), out_grad
    )
    half = mine + lax.ppermute(other, "core", swap)
    block = lax.all_to_all(half, ("y", "x"), 0, 0, tiled=True).sum(axis=0)
    block = spread(block, ("zh", "zl"), 16).sum(axis=0)
    half = spread(block, ("y", "x"), GRID)
    weight_grad, bias_grad = unpack(core, half, lax.ppermute(half, "core", swap))
    return activated, weight_grad, bias_grad.reshape(F)


def solution(mesh):
    fine = Mesh(mesh.devices.reshape(8, 4, 4, 4, 2), AXES)
    return jax.shard_map(
        local,
        mesh=fine,
        in_specs=(
            P(AXES, None),
            P(AXES, None),
            P(AXES, None),
            P(AXES),
            P(AXES, None, None, None),
            P(),
            P(),
            P(AXES, None),
        ),
        out_specs=(P(AXES, None), P(), P()),
        check_vma=False,
    )
```
